128 devices in a mesh: row: 8 (over y, core), col: 16 (over z, x).
Axes of the slice: x: 4, y: 4, z: 4, core: 2. Of those that a mesh axis runs over, the one named last changes fastest.
Arguments:
- children: float32 [12288, 6144], P('row', 'col'), may hold values from -6 to 6
- permutation: int32 [12288], replicated, may hold values from 0 to 12287, as said below
- type_counts: int32 [4], replicated, may hold values from 768 to 6144, as said below
- rotation: float32 [12288], replicated, may hold values from -3.140625 to 3.140625
- pole_values: float32 [12288], replicated, may hold values from -0.15 to 12287.15, as said below
- coupling: float32 [12288], replicated, may hold values from -3 to 3, as said below
- root_gap: int32 [4096], replicated, may hold values from 0 to 6142, as said below
- root_offset: float32 [4096], replicated, may hold values from 0.3 to 0.4
Outputs:
- merged: float32 [4096, 12288], P('col', 'row')
The draws below stay inside these ranges and needn't reach their ends.
Inputs may be any that keep to these rules, and one draw needn't show every extreme that they name: A permutation of 0 to 12287. permutation[j] < 6144 for j < type_counts[0] + type_counts[1]; permutation[j] >= 6144 for type_counts[0] + type_counts[1] <= j < live; for every dense joint column j, the value permutation[j] + 6144 stands at some deflated position. The four counts sum to 12288; type_counts[1] lies in 768 to 1536; the smaller of type_counts[0] and type_counts[2] equals 1536; the larger of type_counts[0] + type_counts[1] and type_counts[1] + type_counts[2] equals 4608; type_counts[3] equals 6144. pole_values[j] lies within 0.15 of j. `coupling`: every entry has magnitude 0.3 or more. `root_gap`: distinct values.
All inputs are finite; a program needn't handle non-finite values.
Results may differ from the reference program's by a relative error of at most 0.00007.
Values sent between devices are 32-bit elements; how exact they have to be, the bound alone decides.
No kernel may reach another device: no remote copies, remote signals or barrier semaphores. Data moves between devices by JAX's collectives and lax.ppermute only.
A program may use at most 64 MiB of HBM per device.

```python
import jax
import jax.numpy as jnp
from jax import lax

N = 12288
HALF = 6144
ROOTS = 4096


def deflation_plan(key):
    key_list = jax.random.split(jax.random.fold_in(key, 11), 5)
    half_size = N // 2
    dense_count = jax.random.randint(key_list[0], (), N // 16, N // 8 + 1, dtype=jnp.int32)
    busy_count = 3 * N // 8 - dense_count
    other_count = jnp.int32(N // 8)
    flip_bit = jax.random.randint(key_list[2], (), 0, 2, dtype=jnp.int32)
    upper_only = jnp.where(flip_bit == 1, busy_count, other_count)
    lower_count = jnp.where(flip_bit == 1, other_count, busy_count)
    deflated_count = N - upper_only - dense_count - lower_count
    order_top = jax.random.permutation(key_list[3], half_size).astype(jnp.int32)
    rank_top = jnp.argsort(order_top, stable=True).astype(jnp.int32)
    paired = (rank_top >= upper_only) & (rank_top < upper_only + dense_count)
    scores = paired.astype(jnp.int32) * half_size + jax.random.permutation(key_list[4], half_size).astype(jnp.int32)
    order_low = jnp.argsort(scores, stable=True).astype(jnp.int32)
    position = jnp.arange(N, dtype=jnp.int32)
    upper_count = upper_only + dense_count
    live_count = upper_count + lower_count
    spare_top = half_size - upper_count
    tail_index = position - live_count
    pick_top = jnp.clip(position, 0, half_size - 1)
    pick_low = jnp.clip(position - upper_count, 0, half_size - 1)
    pick_spare = jnp.clip(upper_count + tail_index, 0, half_size - 1)
    pick_rest = jnp.clip(lower_count + tail_index - spare_top, 0, half_size - 1)
    result = jnp.where(position < upper_count, order_top[pick_top], jnp.where(position < live_count, half_size + order_low[pick_low], jnp.where(tail_index < spare_top, order_top[pick_spare], half_size + order_low[pick_rest])))
    totals = jnp.stack([upper_only, dense_count, lower_count, deflated_count]).astype(jnp.int32)
    return (result.astype(jnp.int32), totals)


def draw_permutation(key, part):
    return deflation_plan(key)[0]


def draw_type_counts(key, part):
    return deflation_plan(key)[1]


def draw_pole_values(key, part):
    key_list = jax.random.split(jax.random.fold_in(key, 23), 2)
    position = jnp.arange(N).astype(jnp.float32)
    jitter = jax.random.uniform(key_list[1], (N,), jnp.float32, -0.15, 0.15)
    return position + jitter


def draw_coupling(key, part):
    key_list = jax.random.split(jax.random.fold_in(key, 37), 2)
    sign_flip = 2.0 * jax.random.bernoulli(key_list[0], 0.5, (N,)).astype(jnp.float32) - 1.0
    magnitude = jnp.exp(jax.random.uniform(key_list[1], (N,), jnp.float32, jnp.log(0.3), jnp.log(3.0)))
    return sign_flip * magnitude


def draw_root_gap(key, part):
    chosen = jax.random.permutation(jax.random.fold_in(key, 5), N // 2 - 1)
    return chosen[:ROOTS].astype(jnp.int32)


def level_of(key, extent, cuts, low, high):
    level = 1.0
    for axis_at, parts in cuts:
        draws = jax.random.uniform(jax.random.fold_in(jax.random.fold_in(key, 6), axis_at), (parts,), jnp.float32, low / len(cuts), high / len(cuts))
        level = level * jnp.repeat(jnp.exp(draws), extent[axis_at] // parts).reshape((-1,) + (1,) * (len(extent) - 1 - axis_at))
    return level


def centred(own_key, extent, deviation, bound, cuts=(), held_as=jnp.bfloat16):
    values = jax.random.normal(own_key, extent, jnp.float32) * deviation
    if len(cuts) > 0:
        values = level_of(own_key, extent, cuts, -0.22, 0.18) * values
    return jnp.clip(values, min=-bound, max=bound).astype(held_as)


def setup_inputs(seed: int = 0) -> dict:
    streams_of = jax.random.split(jax.random.key(seed), 9)
    return {
        "children": centred(streams_of[0], (N, HALF), 1.0, 6.0, ((0, 8), (1, 16)), jnp.float32),
        "permutation": draw_permutation(jax.random.fold_in(streams_of[8], 71), 0),
        "type_counts": draw_type_counts(jax.random.fold_in(streams_of[8], 71), 0),
        "rotation": jnp.clip(jax.random.uniform(streams_of[3], (N,), jnp.float32, -3.140625, 3.140625), -3.140625, 3.140625),
        "pole_values": draw_pole_values(jax.random.fold_in(streams_of[8], 71), 0),
        "coupling": draw_coupling(jax.random.fold_in(streams_of[8], 71), 0),
        "root_gap": draw_root_gap(jax.random.fold_in(streams_of[8], 71), 0),
        "root_offset": jnp.clip(jax.random.uniform(streams_of[7], (ROOTS,), jnp.float32, 0.3, 0.4), 0.3, 0.4),
    }


EPSILON = 1e-06
EXACT = lax.Precision.HIGHEST

def reference(children, permutation, type_counts, rotation, pole_values, coupling, root_gap, root_offset):
    half_size = N // 2
    joint_index = jnp.arange(N, dtype=jnp.int32)
    upper_end = type_counts[0]
    dense_end = type_counts[0] + type_counts[1]
    live_count = dense_end + type_counts[2]
    source = jnp.where(permutation >= half_size, permutation - half_size, permutation).astype(jnp.int32)
    paired = (joint_index >= upper_end) & (joint_index < dense_end)
    lower_only = (joint_index >= dense_end) & (joint_index < live_count)
    zero_fill = jnp.zeros_like(rotation)
    one_fill = jnp.ones_like(rotation)
    upper_factor = jnp.where(joint_index < upper_end, one_fill, jnp.where(paired, jnp.cos(rotation), zero_fill))
    lower_factor = jnp.where(paired, jnp.sin(rotation), jnp.where(lower_only, one_fill, zero_fill))
    base_poles = pole_values[root_gap]
    gap_diff = pole_values[:, None] - base_poles[None, :] - root_offset[None, :]
    cauchy = coupling[:, None] / gap_diff
    cauchy = jnp.where((joint_index < live_count)[:, None], cauchy, jnp.zeros_like(cauchy))
    norm_values = jnp.sqrt(lax.optimization_barrier(jnp.sum(cauchy * cauchy, axis=0)) + EPSILON)
    unit_cauchy = cauchy / norm_values[None, :]
    upper_rows = children[:half_size][:, source] * upper_factor[None, :]
    merged_upper = lax.dot_general(unit_cauchy, upper_rows, (((0,), (1,)), ((), ())), precision=EXACT, preferred_element_type=jnp.float32)
    lower_rows = children[half_size:][:, source] * lower_factor[None, :]
    merged_lower = lax.dot_general(unit_cauchy, lower_rows, (((0,), (1,)), ((), ())), precision=EXACT, preferred_element_type=jnp.float32)
    return jnp.concatenate([merged_upper, merged_lower], axis=1)
```

```python
import functools

import jax
import jax.numpy as jnp
from jax import lax
from jax.experimental import pallas as pl
from jax.experimental.pallas import tpu as pltpu
from jax.sharding import PartitionSpec as P

EPSILON = 1e-06
LANES = 128
CHUNK = 768
ROOT_TILE = 512
F32 = jnp.float32
BF16 = jnp.bfloat16


def product(left, right):
    return lax.dot_general(left, right, (((1,), (0,)), ((), ())), preferred_element_type=F32)


def product_lanes(left, right):
    return lax.dot_general(left, right, (((1,), (1,)), ((), ())), preferred_element_type=F32)


def split_two(value):
    high = value.astype(BF16)
    return high, (value - high.astype(F32)).astype(BF16)


def split_three(value):
    high = value.astype(BF16)
    rest = value - high.astype(F32)
    middle = rest.astype(BF16)
    return high, middle, (rest - middle.astype(F32)).astype(BF16)


def inverse_of(gap):
    first = pltpu.reciprocal(gap, approx=True)
    return first * (2.0 - gap * first)


def prep_kernel(
    source, used, amount, pole_row, coupling_row, table, gap_mine, gap_own, offset_own,
    column_scale, pole_wide, base_mine, root_scale,
):
    live = source.shape[1]
    groups = live // LANES
    place = source[...]
    high_place = place // LANES
    low_place = place - high_place * LANES
    row_hit = (
        lax.broadcasted_iota(jnp.int32, (groups, live), 0) == high_place
    ) & (used[...] > 0.0)
    low_hit = jnp.where(
        lax.broadcasted_iota(jnp.int32, (LANES, live), 0) == low_place, 1.0, 0.0
    ).astype(BF16)
    spread = []
    for values in (pole_row[...], amount[...]):
        total = None
        for piece in split_three(values):
            left = jnp.where(row_hit, piece.astype(F32), 0.0).astype(BF16)
            part = product_lanes(left, low_hit)
            total = part if total is None else total + part
        spread.append(total)
    column_scale[...] = spread[1]
    for group in range(groups):
        row = spread[0][group : group + 1, :]
        pole_wide[group * LANES : (group + 1) * LANES, :] = jnp.broadcast_to(
            row, (LANES, LANES)
        ).T

    def look_up(index_row):
        count = index_row.shape[1]
        high_index = index_row // LANES
        low_index = index_row - high_index * LANES
        hit = jnp.where(
            lax.broadcasted_iota(jnp.int32, (groups, count), 0) == high_index, 1.0, 0.0
        ).astype(BF16)
        total = None
        for piece in split_three(table[...]):
            part = product(piece, hit)
            total = part if total is None else total + part
        chosen = lax.broadcasted_iota(jnp.int32, (LANES, count), 0) == low_index
        return jnp.sum(jnp.where(chosen, total, 0.0), axis=0, keepdims=True)

    base_mine[...] = look_up(gap_mine[...])
    base_own = look_up(gap_own[...])
    for part in range(gap_own.shape[1] // LANES):
        lanes = slice(part * LANES, (part + 1) * LANES)
        base_tall = jnp.broadcast_to(base_own[:, lanes], (LANES, LANES)).T
        offset_tall = jnp.broadcast_to(offset_own[:, lanes], (LANES, LANES)).T
        total = jnp.zeros((LANES, LANES), F32)
        for group in range(groups):
            where = slice(group * LANES, (group + 1) * LANES)
            gap = (pole_row[:, where] - base_tall) - offset_tall
            entry = coupling_row[:, where] * inverse_of(gap)
            total = total + entry * entry
        root_scale[lanes, :] = lax.rsqrt(jnp.sum(total, axis=1, keepdims=True) + EPSILON)


def merge_kernel(
    mine, other, column_scale, pole_wide, base, offset, out_mine, out_other, pieces
):
    sources, band, width = mine.shape
    depth = sources * width
    roots = base.shape[1]
    per_source = width // LANES
    for source in range(sources):
        for part in range(per_source):
            lanes = slice(part * LANES, (part + 1) * LANES)
            at = slice(source * width + part * LANES, source * width + (part + 1) * LANES)
            row = source * per_source + part
            scale = column_scale[row : row + 1, :]
            for half, ref in enumerate((mine, other)):
                high, low = split_two(ref[source, :, lanes] * scale)
                pieces[half * band : (half + 1) * band, at] = high
                pieces[(2 + half) * band : (3 + half) * band, at] = low

    def one_tile(tile, carry):
        first = pl.multiple_of(tile * ROOT_TILE, ROOT_TILE)
        base_row = base[:, pl.ds(first, ROOT_TILE)]
        offset_row = offset[:, pl.ds(first, ROOT_TILE)]
        total = None
        for start in range(0, depth, CHUNK):
            poles = pole_wide[start : start + CHUNK, :]
            highs = []
            lows = []
            for part in range(ROOT_TILE // LANES):
                lanes = slice(part * LANES, (part + 1) * LANES)
                gap = (poles - base_row[:, lanes]) - offset_row[:, lanes]
                near = pltpu.reciprocal(gap, approx=True)
                high = near.astype(BF16)
                lows.append(((1.0 - gap * high.astype(F32)) * near).astype(BF16))
                highs.append(high)
            both = product(pieces[:, start : start + CHUNK], jnp.concatenate(highs, axis=1))
            rest = product(
                pieces[: 2 * band, start : start + CHUNK], jnp.concatenate(lows, axis=1)
            )
            part = both[: 2 * band] + both[2 * band :] + rest
            total = part if total is None else total + part
        for part in range(ROOT_TILE // LANES):
            lanes = slice(part * LANES, (part + 1) * LANES)
            block = tile * (ROOT_TILE // LANES) + part
            out_mine[block] = total[:band, lanes]
            out_other[block] = total[band:, lanes]
        return carry

    lax.fori_loop(0, roots // ROOT_TILE, one_tile, 0)


def finish_kernel(core, mine, other, root_scale, merged):
    sources, band, width = mine.shape
    for which, ref in ((core[0], mine), (1 - core[0], other)):
        rows = pl.ds(pl.multiple_of(which * width, width), width)
        scale = root_scale[rows, :]
        merged[rows, :] = ref[...].reshape(sources * band, width).T * scale


def vmem(count):
    return [pl.BlockSpec(memory_space=pltpu.VMEM)] * count


def per_device(
    children, permutation, type_counts, rotation, pole_values, coupling, root_gap, root_offset
):
    order_size = permutation.shape[0]
    half_size = order_size // 2
    groups = lax.axis_size("col")
    position = lax.axis_index("col")
    row_index = lax.axis_index("row")
    rows = lax.axis_size("row")
    core = row_index % 2
    is_upper = row_index < rows // 2
    root_count = root_gap.shape[0]
    share = root_count // groups
    band = children.shape[0] // groups
    width = children.shape[1]
    pairs = [(index, index ^ 1) for index in range(rows)]

    received = lax.all_to_all(
        children.reshape(groups, band, width), "col", split_axis=0, concat_axis=0, tiled=True
    )

    joint_index = jnp.arange(half_size, dtype=jnp.int32)
    upper_end = type_counts[0]
    dense_end = type_counts[0] + type_counts[1]
    live_count = dense_end + type_counts[2]
    paired = (joint_index >= upper_end) & (joint_index < dense_end)
    lower_only = (joint_index >= dense_end) & (joint_index < live_count)
    angle = rotation[:half_size]
    upper_part = jnp.where(joint_index < upper_end, 1.0, jnp.where(paired, jnp.cos(angle), 0.0))
    lower_part = jnp.where(paired, jnp.sin(angle), jnp.where(lower_only, 1.0, 0.0))
    factor = jnp.where(is_upper, upper_part, lower_part)
    used = jnp.where(
        jnp.where(is_upper, joint_index < dense_end, paired | lower_only), 1.0, 0.0
    )
    live_coupling = jnp.where(joint_index < live_count, coupling[:half_size], 0.0)
    order = permutation[:half_size]
    source = jnp.where(order >= half_size, order - half_size, order)
    poles = pole_values[:half_size]
    gap_blocks = root_gap.reshape(groups, 2, share // 2)
    offset_blocks = root_offset.reshape(groups, 2, share // 2)
    gap_mine = lax.dynamic_index_in_dim(gap_blocks, core, 1, keepdims=False).reshape(1, -1)
    offset_mine = lax.dynamic_index_in_dim(offset_blocks, core, 1, keepdims=False).reshape(1, -1)
    gap_own = lax.dynamic_slice_in_dim(root_gap, position * share, share).reshape(1, -1)
    offset_own = lax.dynamic_slice_in_dim(root_offset, position * share, share).reshape(1, -1)

    column_scale, pole_wide, base_mine, root_scale = pl.pallas_call(
        prep_kernel,
        out_shape=(
            jax.ShapeDtypeStruct((half_size // LANES, LANES), F32),
            jax.ShapeDtypeStruct((half_size, LANES), F32),
            jax.ShapeDtypeStruct((1, root_count // 2), F32),
            jax.ShapeDtypeStruct((share, 1), F32),
        ),
        in_specs=vmem(9),
        out_specs=tuple(vmem(4)),
        compiler_params=pltpu.CompilerParams(vmem_limit_bytes=40 * 2**20),
        cost_estimate=pl.CostEstimate(
            flops=2 * 10**9, bytes_accessed=4 * 10**6, transcendentals=2 * 10**6
        ),
    )(
        source.reshape(1, -1),
        used.reshape(1, -1),
        (live_coupling * factor).reshape(1, -1),
        poles.reshape(1, -1),
        live_coupling.reshape(1, -1),
        poles.reshape(-1, LANES).T,
        gap_mine,
        gap_own,
        offset_own,
    )

    swapped = lax.ppermute(received, "row", pairs)
    piece = jax.ShapeDtypeStruct((groups, band, share // 2), F32)
    out_mine, out_other = pl.pallas_call(
        merge_kernel,
        out_shape=(piece, piece),
        in_specs=vmem(6),
        out_specs=tuple(vmem(2)),
        scratch_shapes=[pltpu.VMEM((4 * band, groups * width), BF16)],
        compiler_params=pltpu.CompilerParams(vmem_limit_bytes=48 * 2**20),
        cost_estimate=pl.CostEstimate(
            flops=30 * 10**9, bytes_accessed=10 * 10**6, transcendentals=12 * 10**6
        ),
    )(received, swapped, column_scale, pole_wide, base_mine, offset_mine)

    def exchange(value):
        return lax.all_to_all(value, "col", split_axis=0, concat_axis=0, tiled=True)

    done_mine = exchange(out_mine)
    done_other = exchange(lax.ppermute(out_other, "row", pairs))
    return pl.pallas_call(
        finish_kernel,
        out_shape=jax.ShapeDtypeStruct((share, groups * band), F32),
        in_specs=[pl.BlockSpec(memory_space=pltpu.SMEM)] + vmem(3),
        out_specs=pl.BlockSpec(memory_space=pltpu.VMEM),
        compiler_params=pltpu.CompilerParams(vmem_limit_bytes=32 * 2**20),
    )(core.reshape(1), done_mine, done_other, root_scale)


def solution(mesh):
    placed = (P("row", "col"), P(), P(), P(), P(), P(), P(), P())
    return jax.shard_map(
        per_device, mesh=mesh, in_specs=placed, out_specs=P("col", "row"), check_vma=False
    )
```

```python
import functools

import jax
import jax.numpy as jnp
from jax import lax
from jax.experimental import pallas as pl
from jax.experimental.pallas import tpu as pltpu
from jax.sharding import PartitionSpec as P

EPSILON = 1e-06
LANES = 128
CHUNK = 1024
ROOT_TILE = 512
F32 = jnp.float32
BF16 = jnp.bfloat16


def product(left, right):
    return lax.dot_general(left, right, (((1,), (0,)), ((), ())), preferred_element_type=F32)


def product_lanes(left, right):
    return lax.dot_general(left, right, (((1,), (1,)), ((), ())), preferred_element_type=F32)


def split_two(value):
    high = value.astype(BF16)
    return high, (value - high.astype(F32)).astype(BF16)


def split_three(value):
    high = value.astype(BF16)
    rest = value - high.astype(F32)
    middle = rest.astype(BF16)
    return high, middle, (rest - middle.astype(F32)).astype(BF16)


def inverse_of(gap):
    first = pltpu.reciprocal(gap, approx=True)
    return first * (2.0 - gap * first)


def prep_kernel(
    counts, core, position, row_index, rows_total, permutation, rotation, pole_values, coupling,
    root_gap, root_offset, column_scale, pole_wide, rows, root_scale, gap_mine, table,
):
    live = permutation.shape[1] // 2
    share = root_scale.shape[0]
    blocks = root_gap.shape[1] // share
    joint = lax.broadcasted_iota(jnp.int32, (1, live), 1)
    upper_end = counts[0]
    dense_end = upper_end + counts[1]
    live_count = dense_end + counts[2]
    paired = (joint >= upper_end) & (joint < dense_end)
    lower_only = (joint >= dense_end) & (joint < live_count)
    angle = rotation[:, :live]
    upper_part = jnp.where(joint < upper_end, 1.0, jnp.where(paired, jnp.cos(angle), 0.0))
    lower_part = jnp.where(paired, jnp.sin(angle), jnp.where(lower_only, 1.0, 0.0))
    upper_used = jnp.where(joint < dense_end, 1.0, 0.0)
    lower_used = jnp.where(paired | lower_only, 1.0, 0.0)
    is_upper = row_index[0] < rows_total[0] // 2
    factor = jnp.where(is_upper, upper_part, lower_part)
    used = jnp.where(is_upper, upper_used, lower_used)
    coupling_row = jnp.where(joint < live_count, coupling[:, :live], 0.0)
    pole_row = pole_values[:, :live]
    order = permutation[:, :live]
    place = jnp.where(order >= live, order - live, order)
    groups = live // LANES
    high_place = place // LANES
    low_place = place - high_place * LANES
    row_hit = (
        lax.broadcasted_iota(jnp.int32, (groups, live), 0) == high_place
    ) & (used > 0.0)
    low_hit = jnp.where(
        lax.broadcasted_iota(jnp.int32, (LANES, live), 0) == low_place, 1.0, 0.0
    ).astype(BF16)
    pieces = [
        jnp.where(row_hit, piece.astype(F32), 0.0).astype(BF16)
        for values in (pole_row, coupling_row * factor)
        for piece in split_three(values)
    ]
    spread = product_lanes(jnp.concatenate(pieces, axis=0), low_hit)
    placed = [
        (spread[first : first + groups] + spread[first + groups : first + 2 * groups])
        + spread[first + 2 * groups : first + 3 * groups]
        for first in (0, 3 * groups)
    ]
    column_scale[...] = placed[1]
    for group in range(groups):
        pole_wide[group * LANES : (group + 1) * LANES, :] = jnp.broadcast_to(
            placed[0][group : group + 1, :], (LANES, LANES)
        ).T
    table[...] = jnp.zeros_like(table)
    for group in range(groups):
        table[group : group + 1, :] = pole_row[:, group * LANES : (group + 1) * LANES]
    table_pieces = split_three(table[...].T)

    def look_up(index_row):
        count = index_row.shape[1]
        high_index = index_row // LANES
        low_index = index_row - high_index * LANES
        hit = jnp.where(
            lax.broadcasted_iota(jnp.int32, (LANES, count), 0) == high_index, 1.0, 0.0
        ).astype(BF16)
        total = None
        for piece in table_pieces:
            part = product(piece, hit)
            total = part if total is None else total + part
        chosen = lax.broadcasted_iota(jnp.int32, (LANES, count), 0) == low_index
        return jnp.sum(jnp.where(chosen, total, 0.0), axis=0, keepdims=True)

    half_share = share // 2
    for block in range(blocks):
        lanes = pl.ds(pl.multiple_of(block * share + core[0] * half_share, LANES), half_share)
        here = slice(block * half_share, (block + 1) * half_share)
        gap_mine[:, here] = root_gap[:, lanes]
        rows[1:2, here] = root_offset[:, lanes]
    rows[0:1, :] = look_up(gap_mine[...])
    own = pl.ds(pl.multiple_of(position[0] * share, LANES), share)
    base_own = look_up(root_gap[:, own])
    offset_own = root_offset[:, own]
    for part in range(share // LANES):
        lanes = slice(part * LANES, (part + 1) * LANES)
        base_tall = jnp.broadcast_to(base_own[:, lanes], (LANES, LANES)).T
        offset_tall = jnp.broadcast_to(offset_own[:, lanes], (LANES, LANES)).T
        total = jnp.zeros((LANES, LANES), F32)
        for group in range(groups):
            where = slice(group * LANES, (group + 1) * LANES)
            gap = (pole_row[:, where] - base_tall) - offset_tall
            entry = coupling_row[:, where] * inverse_of(gap)
            total = total + entry * entry
        root_scale[lanes, :] = lax.rsqrt(jnp.sum(total, axis=1, keepdims=True) + EPSILON)


def merge_kernel(core, mine, other, column_scale, pole_wide, rows, out, pieces):
    groups, band, width = mine.shape
    parts = width // LANES
    depth = groups * width
    tiles = rows.shape[1] // ROOT_TILE
    per_tile = ROOT_TILE // LANES
    for half, ref in enumerate((mine, other)):
        for source in range(groups):
            for part in range(parts):
                lanes = slice(part * LANES, (part + 1) * LANES)
                first = source * width + part * LANES
                at = slice(first, first + LANES)
                row = source * parts + part
                high, low = split_two(ref[source, :, lanes] * column_scale[row : row + 1, :])
                pieces[half * band : (half + 1) * band, at] = high
                pieces[(2 + half) * band : (3 + half) * band, at] = low

    def one_tile(tile, carry):
        first = pl.multiple_of(tile * ROOT_TILE, ROOT_TILE)
        base_row = rows[0:1, pl.ds(first, ROOT_TILE)]
        offset_row = rows[1:2, pl.ds(first, ROOT_TILE)]
        total = None
        for start in range(0, depth, CHUNK):
            column = pole_wide[start : start + CHUNK, :]
            highs = []
            lows = []
            for part in range(per_tile):
                lanes = slice(part * LANES, (part + 1) * LANES)
                gap = (column - base_row[:, lanes]) - offset_row[:, lanes]
                high = pltpu.reciprocal(gap, approx=True).astype(BF16)
                lows.append((1.0 - gap * high.astype(F32)).astype(BF16) * high)
                highs.append(high)
            both = product(pieces[:, start : start + CHUNK], jnp.concatenate(highs, axis=1))
            rest = product(
                pieces[: 2 * band, start : start + CHUNK], jnp.concatenate(lows, axis=1)
            )
            part = both[: 2 * band] + both[2 * band :] + rest
            total = part if total is None else total + part
        for half, which in enumerate((core[0], 1 - core[0])):
            for part in range(per_tile):
                lanes = slice(part * LANES, (part + 1) * LANES)
                block = which * groups + tile * per_tile + part
                out[block] = total[half * band : (half + 1) * band, lanes]
        return carry

    lax.fori_loop(0, tiles, one_tile, 0)


def finish_kernel(blocks, root_scale, merged, made, sems):
    sources, band, width = blocks.shape
    groups = sources // 2
    copies = []
    for half in range(2):
        rows = pl.ds(half * width, width)
        tall = blocks[half * groups : (half + 1) * groups].reshape(groups * band, width)
        made[rows, :] = tall.T * root_scale[rows, :]
        copies.append(pltpu.make_async_copy(made.at[rows], merged.at[rows], sems.at[half]))
        copies[half].start()
    for copy in copies:
        copy.wait()


def hbm(count):
    return [pl.BlockSpec(memory_space=pltpu.HBM)] * count


def vmem(count):
    return [pl.BlockSpec(memory_space=pltpu.VMEM)] * count


def per_device(
    children, permutation, type_counts, rotation, pole_values, coupling, root_gap, root_offset
):
    order_size = permutation.shape[0]
    half_size = order_size // 2
    groups = lax.axis_size("col")
    position = lax.axis_index("col")
    row_index = lax.axis_index("row")
    rows = lax.axis_size("row")
    core = row_index % 2
    is_upper = row_index < rows // 2
    root_count = root_gap.shape[0]
    share = root_count // groups
    band = children.shape[0] // groups
    width = children.shape[1]
    pairs = [(index, index ^ 1) for index in range(rows)]

    mine = lax.all_to_all(
        children.reshape(groups, band, width), "col", split_axis=0, concat_axis=0, tiled=True
    )
    mine, permutation = lax.optimization_barrier((mine, permutation))
    other = lax.ppermute(mine, "row", pairs)
    column_scale, pole_wide, root_rows, root_scale = pl.pallas_call(
        prep_kernel,
        out_shape=(
            jax.ShapeDtypeStruct((half_size // LANES, LANES), F32),
            jax.ShapeDtypeStruct((half_size, LANES), F32),
            jax.ShapeDtypeStruct((2, root_count // 2), F32),
            jax.ShapeDtypeStruct((share, 1), F32),
        ),
        in_specs=[pl.BlockSpec(memory_space=pltpu.SMEM)] * 5 + vmem(6),
        out_specs=tuple(vmem(4)),
        scratch_shapes=[
            pltpu.VMEM((1, root_count // 2), jnp.int32),
            pltpu.VMEM((LANES, LANES), F32),
        ],
        compiler_params=pltpu.CompilerParams(vmem_limit_bytes=32 * 2**20),
        cost_estimate=pl.CostEstimate(
            flops=4 * 10**9, bytes_accessed=4 * 10**6, transcendentals=2 * 10**6
        ),
    )(
        type_counts,
        core.reshape(1),
        position.reshape(1),
        row_index.reshape(1),
        jnp.full((1,), rows, jnp.int32),
        *(
            value.reshape(1, -1)
            for value in (permutation, rotation, pole_values, coupling, root_gap, root_offset)
        ),
    )
    blocks = pl.pallas_call(
        merge_kernel,
        out_shape=jax.ShapeDtypeStruct((2 * groups, band, share // 2), F32),
        in_specs=[pl.BlockSpec(memory_space=pltpu.SMEM)] + vmem(5),
        out_specs=vmem(1)[0],
        scratch_shapes=[pltpu.VMEM((4 * band, groups * width), BF16)],
        compiler_params=pltpu.CompilerParams(vmem_limit_bytes=32 * 2**20),
        cost_estimate=pl.CostEstimate(
            flops=30 * 10**9, bytes_accessed=10 * 10**6, transcendentals=12 * 10**6
        ),
    )(core.reshape(1), mine, other, column_scale, pole_wide, root_rows)
    chips = [
        [(pair * 2 + half) * groups + index for half in range(2) for index in range(groups)]
        for pair in range(rows // 2)
    ]
    blocks = lax.all_to_all(
        blocks, ("row", "col"), split_axis=0, concat_axis=0, axis_index_groups=chips, tiled=True
    )
    return pl.pallas_call(
        finish_kernel,
        out_shape=jax.ShapeDtypeStruct((share, groups * band), F32),
        in_specs=vmem(2),
        out_specs=hbm(1)[0],
        scratch_shapes=[
            pltpu.VMEM((share, groups * band), F32),
            pltpu.SemaphoreType.DMA((2,)),
        ],
        compiler_params=pltpu.CompilerParams(vmem_limit_bytes=16 * 2**20),
    )(blocks, root_scale)


def solution(mesh):
    placed = (P("row", "col"), P(), P(), P(), P(), P(), P(), P())
    return jax.shard_map(
        per_device, mesh=mesh, in_specs=placed, out_specs=P("col", "row"), check_vma=False
    )
```

```python
import functools

import jax
import jax.numpy as jnp
from jax import lax
from jax.experimental import pallas as pl
from jax.experimental.pallas import tpu as pltpu
from jax.sharding import PartitionSpec as P

EPSILON = 1e-06
LANES = 128
CHUNK = 256
ROOT_TILE = 512
F32 = jnp.float32
BF16 = jnp.bfloat16


def product(left, right):
    return lax.dot_general(left, right, (((1,), (0,)), ((), ())), preferred_element_type=F32)


def product_lanes(left, right):
    return lax.dot_general(left, right, (((1,), (1,)), ((), ())), preferred_element_type=F32)


def split_two(value):
    high = value.astype(BF16)
    return high, (value - high.astype(F32)).astype(BF16)


def split_three(value):
    high = value.astype(BF16)
    rest = value - high.astype(F32)
    middle = rest.astype(BF16)
    return high, middle, (rest - middle.astype(F32)).astype(BF16)


def inverse_of(gap):
    first = pltpu.reciprocal(gap, approx=True)
    return first * (2.0 - gap * first)


def prep_kernel(
    counts, core, position, row_index, rows_total, permutation, rotation, pole_values, coupling,
    root_gap, root_offset, column_scale, pole_wide, rows, root_scale, coupling_live, packed,
    packed_row, place_row, gaps,
):
    groups = permutation.shape[0] // 2
    live = groups * LANES
    share = root_scale.shape[0]
    parts = share // LANES
    shape = (groups, LANES)
    joint = lax.broadcasted_iota(jnp.int32, shape, 0) * LANES + lax.broadcasted_iota(
        jnp.int32, shape, 1
    )
    upper_end = counts[0]
    dense_end = upper_end + counts[1]
    live_count = dense_end + counts[2]
    paired = (joint >= upper_end) & (joint < dense_end)
    lower_only = (joint >= dense_end) & (joint < live_count)
    angle = rotation[:groups]
    upper_part = jnp.where(joint < upper_end, 1.0, jnp.where(paired, jnp.cos(angle), 0.0))
    lower_part = jnp.where(paired, jnp.sin(angle), jnp.where(lower_only, 1.0, 0.0))
    upper_used = jnp.where(joint < dense_end, 1, 0)
    lower_used = jnp.where(paired | lower_only, 1, 0)
    is_upper = row_index[0] < rows_total[0] // 2
    factor = jnp.where(is_upper, upper_part, lower_part)
    used = jnp.where(is_upper, upper_used, lower_used)
    coupling_live[...] = jnp.where(joint < live_count, coupling[:groups], 0.0)
    order = permutation[:groups]
    place = jnp.where(order >= live, order - live, order)
    packed_place = jnp.where(used > 0, place, -1)
    values = [*split_three(pole_values[:groups]), *split_three(coupling_live[...] * factor)]
    for index, piece in enumerate(values):
        packed[index] = piece.astype(F32)
    for group in range(groups):
        here = slice(group * LANES, (group + 1) * LANES)
        place_row[:, here] = packed_place[group : group + 1, :]
        for index in range(len(values)):
            packed_row[index : index + 1, here] = packed[index, group : group + 1, :]
    row_hit = lax.broadcasted_iota(jnp.int32, (groups, live), 0) == (place_row[...] >> 7)
    low_hit = jnp.where(
        lax.broadcasted_iota(jnp.int32, (LANES, live), 0) == (place_row[...] & 127), 1.0, 0.0
    ).astype(BF16)
    pieces = [
        jnp.where(row_hit, packed_row[index : index + 1, :], 0.0).astype(BF16)
        for index in range(len(values))
    ]
    spread = product_lanes(jnp.concatenate(pieces, axis=0), low_hit)
    placed = [
        (spread[first : first + groups] + spread[first + groups : first + 2 * groups])
        + spread[first + 2 * groups : first + 3 * groups]
        for first in (0, 3 * groups)
    ]
    column_scale[...] = placed[1]
    for group in range(groups):
        pole_wide[group * LANES : (group + 1) * LANES, :] = jnp.broadcast_to(
            placed[0][group : group + 1, :], (LANES, LANES)
        ).T

    blocks = root_gap.shape[0] // parts
    mine = blocks * LANES
    for block in range(blocks):
        here = slice(block * LANES, (block + 1) * LANES)
        row = pl.ds(block * parts + core[0], 1)
        gaps[:, here] = root_gap[row, :]
        rows[1:2, here] = root_offset[row, :]
    for part in range(parts):
        here = slice(mine + part * LANES, mine + (part + 1) * LANES)
        gaps[:, here] = root_gap[pl.ds(position[0] * parts + part, 1), :]
    count = gaps.shape[1]
    hit = jnp.where(
        lax.broadcasted_iota(jnp.int32, (groups, count), 0) == (gaps[...] >> 7), 1.0, 0.0
    ).astype(BF16)
    near = None
    for piece in split_three(pole_values[:groups]):
        part = lax.dot_general(
            piece, hit, (((0,), (0,)), ((), ())), preferred_element_type=F32
        )
        near = part if near is None else near + part
    chosen = lax.broadcasted_iota(jnp.int32, (LANES, count), 0) == (gaps[...] & 127)
    base = jnp.sum(jnp.where(chosen, near, 0.0), axis=0, keepdims=True)
    rows[0:1, :] = base[:, :mine]
    for part in range(parts):
        lanes = slice(mine + part * LANES, mine + (part + 1) * LANES)
        base_tall = jnp.broadcast_to(base[:, lanes], (LANES, LANES)).T
        offset_tall = jnp.broadcast_to(
            root_offset[pl.ds(position[0] * parts + part, 1), :], (LANES, LANES)
        ).T
        total = jnp.zeros((LANES, LANES), F32)
        for group in range(groups):
            gap = (pole_values[group : group + 1, :] - base_tall) - offset_tall
            entry = coupling_live[group : group + 1, :] * inverse_of(gap)
            total = total + entry * entry
        root_scale[part * LANES : (part + 1) * LANES, :] = lax.rsqrt(
            jnp.sum(total, axis=1, keepdims=True) + EPSILON
        )


def merge_kernel(core, mine, other, column_scale, pole_wide, rows, out, pieces, held, sems):
    groups, band, width = mine.shape
    quarter = groups // 4
    copies = []
    for index in range(4):
        block = pl.ds(index * quarter, quarter)
        copies.append(pltpu.make_async_copy(other.at[block], held.at[block], sems.at[index]))
        copies[index].start()
    parts = width // LANES
    depth = groups * width
    tiles = rows.shape[1] // ROOT_TILE
    per_tile = ROOT_TILE // LANES
    for half, ref in enumerate((mine, held)):
        for source in range(groups):
            if half == 1 and source % quarter == 0:
                copies[source // quarter].wait()
            for part in range(parts):
                lanes = slice(part * LANES, (part + 1) * LANES)
                first = source * width + part * LANES
                at = slice(first, first + LANES)
                row = source * parts + part
                high, low = split_two(ref[source, :, lanes] * column_scale[row : row + 1, :])
                pieces[half * band : (half + 1) * band, at] = high
                pieces[(2 + half) * band : (3 + half) * band, at] = low

    def one_tile(tile, carry):
        first = pl.multiple_of(tile * ROOT_TILE, ROOT_TILE)
        base_row = rows[0:1, pl.ds(first, ROOT_TILE)]
        offset_row = rows[1:2, pl.ds(first, ROOT_TILE)]
        total = None
        for start in range(0, depth, CHUNK):
            column = pole_wide[start : start + CHUNK, :]
            highs = []
            lows = []
            for part in range(per_tile):
                lanes = slice(part * LANES, (part + 1) * LANES)
                gap = (column - base_row[:, lanes]) - offset_row[:, lanes]
                high = pltpu.reciprocal(gap, approx=True).astype(BF16)
                lows.append((1.0 - gap * high.astype(F32)).astype(BF16) * high)
                highs.append(high)
            both = product(pieces[:, start : start + CHUNK], jnp.concatenate(highs, axis=1))
            rest = product(
                pieces[: 2 * band, start : start + CHUNK], jnp.concatenate(lows, axis=1)
            )
            part = both[: 2 * band] + both[2 * band :] + rest
            total = part if total is None else total + part
        for half, which in enumerate((core[0], 1 - core[0])):
            for part in range(per_tile):
                lanes = slice(part * LANES, (part + 1) * LANES)
                block = which * groups + tile * per_tile + part
                out[block] = total[half * band : (half + 1) * band, lanes]
        return carry

    lax.fori_loop(0, tiles, one_tile, 0)


def finish_kernel(blocks, root_scale, merged, made, sems):
    sources, band, width = blocks.shape
    groups = sources // 2
    pieces = sems.shape[1]
    step = groups // pieces
    copies = []
    for half in range(2):
        rows = pl.ds(half * width, width)
        for piece in range(pieces):
            first = half * groups + piece * step
            tall = blocks[first : first + step].reshape(step * band, width)
            lanes = pl.ds(piece * step * band, step * band)
            made[rows, lanes] = tall.T * root_scale[rows, :]
            copies.append(
                pltpu.make_async_copy(
                    made.at[rows, lanes], merged.at[rows, lanes], sems.at[half, piece]
                )
            )
            copies[-1].start()
    for copy in copies:
        copy.wait()


def hbm(count):
    return [pl.BlockSpec(memory_space=pltpu.HBM)] * count


def vmem(count):
    return [pl.BlockSpec(memory_space=pltpu.VMEM)] * count


def per_device(
    children, permutation, type_counts, rotation, pole_values, coupling, root_gap, root_offset
):
    order_size = permutation.shape[0]
    half_size = order_size // 2
    groups = lax.axis_size("col")
    position = lax.axis_index("col")
    row_index = lax.axis_index("row")
    rows = lax.axis_size("row")
    core = row_index % 2
    is_upper = row_index < rows // 2
    root_count = root_gap.shape[0]
    share = root_count // groups
    band = children.shape[0] // groups
    width = children.shape[1]
    pairs = [(index, index ^ 1) for index in range(rows)]

    mine = lax.all_to_all(
        children.reshape(groups, band, width), "col", split_axis=0, concat_axis=0, tiled=True
    )
    mine, permutation = lax.optimization_barrier((mine, permutation))
    other = lax.ppermute(mine, "row", pairs)
    column_scale, pole_wide, root_rows, root_scale = pl.pallas_call(
        prep_kernel,
        out_shape=(
            jax.ShapeDtypeStruct((half_size // LANES, LANES), F32),
            jax.ShapeDtypeStruct((half_size, LANES), F32),
            jax.ShapeDtypeStruct((2, root_count // 2), F32),
            jax.ShapeDtypeStruct((share, 1), F32),
        ),
        in_specs=[pl.BlockSpec(memory_space=pltpu.SMEM)] * 5 + vmem(6),
        out_specs=tuple(vmem(4)),
        scratch_shapes=[
            pltpu.VMEM((half_size // LANES, LANES), F32),
            pltpu.VMEM((6, half_size // LANES, LANES), F32),
            pltpu.VMEM((6, half_size), F32),
            pltpu.VMEM((1, half_size), jnp.int32),
            pltpu.VMEM((1, root_count // 2 + share), jnp.int32),
        ],
        compiler_params=pltpu.CompilerParams(vmem_limit_bytes=32 * 2**20),
        cost_estimate=pl.CostEstimate(
            flops=4 * 10**9, bytes_accessed=4 * 10**6, transcendentals=2 * 10**6
        ),
    )(
        type_counts,
        core.reshape(1),
        position.reshape(1),
        row_index.reshape(1),
        jnp.full((1,), rows, jnp.int32),
        *(
            value.reshape(-1, LANES)
            for value in (permutation, rotation, pole_values, coupling, root_gap, root_offset)
        ),
    )
    blocks = pl.pallas_call(
        merge_kernel,
        out_shape=jax.ShapeDtypeStruct((2 * groups, band, share // 2), F32),
        in_specs=[pl.BlockSpec(memory_space=pltpu.SMEM)] + vmem(1) + hbm(1) + vmem(3),
        out_specs=vmem(1)[0],
        scratch_shapes=[
            pltpu.VMEM((4 * band, groups * width), BF16),
            pltpu.VMEM((groups, band, width), F32),
            pltpu.SemaphoreType.DMA((4,)),
        ],
        compiler_params=pltpu.CompilerParams(vmem_limit_bytes=32 * 2**20),
        cost_estimate=pl.CostEstimate(
            flops=30 * 10**9, bytes_accessed=10 * 10**6, transcendentals=12 * 10**6
        ),
    )(core.reshape(1), mine, other, column_scale, pole_wide, root_rows)
    chips = [
        [(pair * 2 + half) * groups + index for half in range(2) for index in range(groups)]
        for pair in range(rows // 2)
    ]
    blocks = lax.all_to_all(
        blocks, ("row", "col"), split_axis=0, concat_axis=0, axis_index_groups=chips, tiled=True
    )
    return pl.pallas_call(
        finish_kernel,
        out_shape=jax.ShapeDtypeStruct((share, groups * band), F32),
        in_specs=vmem(2),
        out_specs=hbm(1)[0],
        scratch_shapes=[
            pltpu.VMEM((share, groups * band), F32),
            pltpu.SemaphoreType.DMA((2, 4)),
        ],
        compiler_params=pltpu.CompilerParams(vmem_limit_bytes=16 * 2**20),
    )(blocks, root_scale)


def solution(mesh):
    placed = (P("row", "col"), P(), P(), P(), P(), P(), P(), P())
    return jax.shard_map(
        per_device, mesh=mesh, in_specs=placed, out_specs=P("col", "row"), check_vma=False
    )
```

```python
import functools

import jax
import jax.numpy as jnp
from jax import lax
from jax.experimental import pallas as pl
from jax.experimental.pallas import tpu as pltpu
from jax.sharding import PartitionSpec as P

EPSILON = 1e-06
LANES = 128
CHUNK = 256
ROOT_TILE = 512
F32 = jnp.float32
BF16 = jnp.bfloat16


def product(left, right):
    return lax.dot_general(left, right, (((1,), (0,)), ((), ())), preferred_element_type=F32)


def product_lanes(left, right):
    return lax.dot_general(left, right, (((1,), (1,)), ((), ())), preferred_element_type=F32)


def split_two(value):
    high = value.astype(BF16)
    return high, (value - high.astype(F32)).astype(BF16)


def split_three(value):
    high = value.astype(BF16)
    rest = value - high.astype(F32)
    middle = rest.astype(BF16)
    return high, middle, (rest - middle.astype(F32)).astype(BF16)


def inverse_of(gap):
    first = pltpu.reciprocal(gap, approx=True)
    return first * (2.0 - gap * first)


def prep_kernel(
    counts, core, position, row_index, rows_total, permutation, rotation, pole_values, coupling,
    root_gap, root_offset, column_scale, pole_wide, rows, root_scale, coupling_live, packed,
    packed_row, place_row, gaps,
):
    groups = permutation.shape[0] // 2
    live = groups * LANES
    parts = root_scale.shape[0]
    shape = (groups, LANES)
    joint = lax.broadcasted_iota(jnp.int32, shape, 0) * LANES + lax.broadcasted_iota(
        jnp.int32, shape, 1
    )
    upper_end = counts[0]
    dense_end = upper_end + counts[1]
    live_count = dense_end + counts[2]
    paired = (joint >= upper_end) & (joint < dense_end)
    lower_only = (joint >= dense_end) & (joint < live_count)
    angle = rotation[:groups]
    upper_part = jnp.where(joint < upper_end, 1.0, jnp.where(paired, jnp.cos(angle), 0.0))
    lower_part = jnp.where(paired, jnp.sin(angle), jnp.where(lower_only, 1.0, 0.0))
    upper_used = jnp.where(joint < dense_end, 1, 0)
    lower_used = jnp.where(paired | lower_only, 1, 0)
    is_upper = row_index[0] < rows_total[0] // 2
    factor = jnp.where(is_upper, upper_part, lower_part)
    used = jnp.where(is_upper, upper_used, lower_used)
    coupling_live[...] = jnp.where(joint < live_count, coupling[:groups], 0.0)
    order = permutation[:groups]
    place = jnp.where(order >= live, order - live, order)
    packed_place = jnp.where(used > 0, place, -1)
    values = [*split_three(pole_values[:groups]), *split_three(coupling_live[...] * factor)]
    for index, piece in enumerate(values):
        packed[index] = piece.astype(F32)
    for group in range(groups):
        here = slice(group * LANES, (group + 1) * LANES)
        place_row[:, here] = packed_place[group : group + 1, :]
        for index in range(len(values)):
            packed_row[index : index + 1, here] = packed[index, group : group + 1, :]
    row_hit = lax.broadcasted_iota(jnp.int32, (groups, live), 0) == (place_row[...] >> 7)
    low_hit = jnp.where(
        lax.broadcasted_iota(jnp.int32, (LANES, live), 0) == (place_row[...] & 127), 1.0, 0.0
    ).astype(BF16)
    pieces = [
        jnp.where(row_hit, packed_row[index : index + 1, :], 0.0).astype(BF16)
        for index in range(len(values))
    ]
    spread = product_lanes(jnp.concatenate(pieces, axis=0), low_hit)
    placed = [
        (spread[first : first + groups] + spread[first + groups : first + 2 * groups])
        + spread[first + 2 * groups : first + 3 * groups]
        for first in (0, 3 * groups)
    ]
    column_scale[...] = placed[1]
    for group in range(groups):
        pole_wide[group * LANES : (group + 1) * LANES, :] = jnp.broadcast_to(
            placed[0][group : group + 1, :], (LANES, LANES)
        ).T

    blocks = root_gap.shape[0] // parts
    mine = blocks * LANES
    for block in range(blocks):
        here = slice(block * LANES, (block + 1) * LANES)
        row = pl.ds(block * parts + core[0], 1)
        gaps[:, here] = root_gap[row, :]
        rows[1:2, here] = root_offset[row, :]
    for part in range(parts):
        here = slice(mine + part * LANES, mine + (part + 1) * LANES)
        gaps[:, here] = root_gap[pl.ds(position[0] * parts + part, 1), :]
    count = gaps.shape[1]
    hit = jnp.where(
        lax.broadcasted_iota(jnp.int32, (groups, count), 0) == (gaps[...] >> 7), 1.0, 0.0
    ).astype(BF16)
    near = None
    for piece in split_three(pole_values[:groups]):
        part = lax.dot_general(
            piece, hit, (((0,), (0,)), ((), ())), preferred_element_type=F32
        )
        near = part if near is None else near + part
    chosen = lax.broadcasted_iota(jnp.int32, (LANES, count), 0) == (gaps[...] & 127)
    base = jnp.sum(jnp.where(chosen, near, 0.0), axis=0, keepdims=True)
    rows[0:1, :] = base[:, :mine]
    for part in range(parts):
        lanes = slice(mine + part * LANES, mine + (part + 1) * LANES)
        base_tall = jnp.broadcast_to(base[:, lanes], (LANES, LANES)).T
        offset_tall = jnp.broadcast_to(
            root_offset[pl.ds(position[0] * parts + part, 1), :], (LANES, LANES)
        ).T
        total = jnp.zeros((LANES, LANES), F32)
        for group in range(groups):
            gap = (pole_values[group : group + 1, :] - base_tall) - offset_tall
            entry = coupling_live[group : group + 1, :] * inverse_of(gap)
            total = total + entry * entry
        root_scale[part : part + 1, :] = lax.rsqrt(
            jnp.sum(total.T, axis=0, keepdims=True) + EPSILON
        )


def merge_kernel(core, mine, other, column_scale, pole_wide, rows, out, pieces, held, sems):
    groups, band, width = mine.shape
    quarter = groups // 4
    copies = []
    for index in range(4):
        block = pl.ds(index * quarter, quarter)
        copies.append(pltpu.make_async_copy(other.at[block], held.at[block], sems.at[index]))
        copies[index].start()
    parts = width // LANES
    depth = groups * width
    tiles = rows.shape[1] // ROOT_TILE
    per_tile = ROOT_TILE // LANES
    for half, ref in enumerate((mine, held)):
        for source in range(groups):
            if half == 1 and source % quarter == 0:
                copies[source // quarter].wait()
            for part in range(parts):
                lanes = slice(part * LANES, (part + 1) * LANES)
                first = source * width + part * LANES
                at = slice(first, first + LANES)
                row = source * parts + part
                high, low = split_two(ref[source, :, lanes] * column_scale[row : row + 1, :])
                pieces[half * band : (half + 1) * band, at] = high
                pieces[(2 + half) * band : (3 + half) * band, at] = low

    def one_tile(tile, carry):
        first = tile * ROOT_TILE
        base_row = rows[0:1, pl.ds(first, ROOT_TILE)]
        offset_row = rows[1:2, pl.ds(first, ROOT_TILE)]
        total = None
        for start in range(0, depth, CHUNK):
            column = pole_wide[start : start + CHUNK, :]
            highs = []
            lows = []
            for part in range(per_tile):
                lanes = slice(part * LANES, (part + 1) * LANES)
                gap = (column - base_row[:, lanes]) - offset_row[:, lanes]
                high = pltpu.reciprocal(gap, approx=True).astype(BF16)
                lows.append((1.0 - gap * high.astype(F32)).astype(BF16) * high)
                highs.append(high)
            both = product(pieces[:, start : start + CHUNK], jnp.concatenate(highs, axis=1))
            rest = product(
                pieces[: 2 * band, start : start + CHUNK], jnp.concatenate(lows, axis=1)
            )
            part = both[: 2 * band] + both[2 * band :] + rest
            total = part if total is None else total + part
        for half, which in enumerate((core[0], 1 - core[0])):
            for part in range(per_tile):
                lanes = slice(part * LANES, (part + 1) * LANES)
                block = which * groups + tile * per_tile + part
                out[block] = total[half * band : (half + 1) * band, lanes]
        return carry

    for tile in range(tiles):
        one_tile(tile, 0)


def finish_kernel(blocks, root_scale, merged, made, sems):
    sources, band, width = blocks.shape
    groups = sources // 2
    pieces = sems.shape[1]
    step = groups // pieces
    copies = []
    for half in range(2):
        rows = pl.ds(half * width, width)
        for piece in range(pieces):
            first = half * groups + piece * step
            tall = blocks[first : first + step].reshape(step * band, width)
            lanes = pl.ds(piece * step * band, step * band)
            made[rows, lanes] = (tall * root_scale[half : half + 1, :]).T
            copies.append(
                pltpu.make_async_copy(
                    made.at[rows, lanes], merged.at[rows, lanes], sems.at[half, piece]
                )
            )
            copies[-1].start()
    for copy in copies:
        copy.wait()


def hbm(count):
    return [pl.BlockSpec(memory_space=pltpu.HBM)] * count


def vmem(count):
    return [pl.BlockSpec(memory_space=pltpu.VMEM)] * count


def per_device(
    children, permutation, type_counts, rotation, pole_values, coupling, root_gap, root_offset
):
    order_size = permutation.shape[0]
    half_size = order_size // 2
    groups = lax.axis_size("col")
    position = lax.axis_index("col")
    row_index = lax.axis_index("row")
    rows = lax.axis_size("row")
    core = row_index % 2
    is_upper = row_index < rows // 2
    root_count = root_gap.shape[0]
    share = root_count // groups
    band = children.shape[0] // groups
    width = children.shape[1]
    pairs = [(index, index ^ 1) for index in range(rows)]

    mine = lax.all_to_all(
        children.reshape(groups, band, width), "col", split_axis=0, concat_axis=0, tiled=True
    )
    mine, permutation = lax.optimization_barrier((mine, permutation))
    other = lax.ppermute(mine, "row", pairs)
    column_scale, pole_wide, root_rows, root_scale = pl.pallas_call(
        prep_kernel,
        out_shape=(
            jax.ShapeDtypeStruct((half_size // LANES, LANES), F32),
            jax.ShapeDtypeStruct((half_size, LANES), F32),
            jax.ShapeDtypeStruct((2, root_count // 2), F32),
            jax.ShapeDtypeStruct((share // LANES, LANES), F32),
        ),
        in_specs=[pl.BlockSpec(memory_space=pltpu.SMEM)] * 5 + vmem(6),
        out_specs=tuple(vmem(4)),
        scratch_shapes=[
            pltpu.VMEM((half_size // LANES, LANES), F32),
            pltpu.VMEM((6, half_size // LANES, LANES), F32),
            pltpu.VMEM((6, half_size), F32),
            pltpu.VMEM((1, half_size), jnp.int32),
            pltpu.VMEM((1, root_count // 2 + share), jnp.int32),
        ],
        compiler_params=pltpu.CompilerParams(vmem_limit_bytes=32 * 2**20),
        cost_estimate=pl.CostEstimate(
            flops=4 * 10**9, bytes_accessed=4 * 10**6, transcendentals=2 * 10**6
        ),
    )(
        type_counts,
        core.reshape(1),
        position.reshape(1),
        row_index.reshape(1),
        jnp.full((1,), rows, jnp.int32),
        *(
            value.reshape(-1, LANES)
            for value in (permutation, rotation, pole_values, coupling, root_gap, root_offset)
        ),
    )
    blocks = pl.pallas_call(
        merge_kernel,
        out_shape=jax.ShapeDtypeStruct((2 * groups, band, share // 2), F32),
        in_specs=[pl.BlockSpec(memory_space=pltpu.SMEM)] + vmem(1) + hbm(1) + vmem(3),
        out_specs=vmem(1)[0],
        scratch_shapes=[
            pltpu.VMEM((4 * band, groups * width), BF16),
            pltpu.VMEM((groups, band, width), F32),
            pltpu.SemaphoreType.DMA((4,)),
        ],
        compiler_params=pltpu.CompilerParams(vmem_limit_bytes=32 * 2**20),
        cost_estimate=pl.CostEstimate(
            flops=30 * 10**9, bytes_accessed=10 * 10**6, transcendentals=12 * 10**6
        ),
    )(core.reshape(1), mine, other, column_scale, pole_wide, root_rows)
    chips = [
        [(pair * 2 + half) * groups + index for half in range(2) for index in range(groups)]
        for pair in range(rows // 2)
    ]
    blocks = lax.all_to_all(
        blocks, ("row", "col"), split_axis=0, concat_axis=0, axis_index_groups=chips, tiled=True
    )
    return pl.pallas_call(
        finish_kernel,
        out_shape=jax.ShapeDtypeStruct((share, groups * band), F32),
        in_specs=vmem(2),
        out_specs=hbm(1)[0],
        scratch_shapes=[
            pltpu.VMEM((share, groups * band), F32),
            pltpu.SemaphoreType.DMA((2, 4)),
        ],
        compiler_params=pltpu.CompilerParams(vmem_limit_bytes=16 * 2**20),
    )(blocks, root_scale)


def solution(mesh):
    placed = (P("row", "col"), P(), P(), P(), P(), P(), P(), P())
    return jax.shard_map(
        per_device, mesh=mesh, in_specs=placed, out_specs=P("col", "row"), check_vma=False
    )
```

```python
import functools

import jax
import jax.numpy as jnp
from jax import lax
from jax.experimental import pallas as pl
from jax.experimental.pallas import tpu as pltpu
from jax.sharding import PartitionSpec as P

EPSILON = 1e-06
LANES = 128
CHUNK = 256
ROOT_TILE = 512
F32 = jnp.float32
BF16 = jnp.bfloat16


def product(left, right):
    return lax.dot_general(left, right, (((1,), (0,)), ((), ())), preferred_element_type=F32)


def product_lanes(left, right):
    return lax.dot_general(left, right, (((1,), (1,)), ((), ())), preferred_element_type=F32)


def split_two(value):
    high = value.astype(BF16)
    return high, (value - high.astype(F32)).astype(BF16)


def split_three(value):
    high = value.astype(BF16)
    rest = value - high.astype(F32)
    middle = rest.astype(BF16)
    return high, middle, (rest - middle.astype(F32)).astype(BF16)


def inverse_of(gap):
    first = pltpu.reciprocal(gap, approx=True)
    return first * (2.0 - gap * first)


def prep_kernel(
    counts, core, position, row_index, rows_total, permutation, rotation, pole_values, coupling,
    root_gap, root_offset, column_scale, pole_wide, rows, root_scale, coupling_live, packed,
    packed_row, place_row, gaps,
):
    groups = permutation.shape[0] // 2
    live = groups * LANES
    parts = 2
    shape = (groups, LANES)
    joint = lax.broadcasted_iota(jnp.int32, shape, 0) * LANES + lax.broadcasted_iota(
        jnp.int32, shape, 1
    )
    upper_end = counts[0]
    dense_end = upper_end + counts[1]
    live_count = dense_end + counts[2]
    paired = (joint >= upper_end) & (joint < dense_end)
    lower_only = (joint >= dense_end) & (joint < live_count)
    angle = rotation[:groups]
    upper_part = jnp.where(joint < upper_end, 1.0, jnp.where(paired, jnp.cos(angle), 0.0))
    lower_part = jnp.where(paired, jnp.sin(angle), jnp.where(lower_only, 1.0, 0.0))
    upper_used = jnp.where(joint < dense_end, 1, 0)
    lower_used = jnp.where(paired | lower_only, 1, 0)
    is_upper = row_index[0] < rows_total[0] // 2
    factor = jnp.where(is_upper, upper_part, lower_part)
    used = jnp.where(is_upper, upper_used, lower_used)
    coupling_live[...] = jnp.where(joint < live_count, coupling[:groups], 0.0)
    order = permutation[:groups]
    place = jnp.where(order >= live, order - live, order)
    packed_place = jnp.where(used > 0, place, -1)
    values = [*split_three(pole_values[:groups]), *split_three(coupling_live[...] * factor)]
    for index, piece in enumerate(values):
        packed[index] = piece.astype(F32)
    for group in range(groups):
        here = slice(group * LANES, (group + 1) * LANES)
        place_row[:, here] = packed_place[group : group + 1, :]
        for index in range(len(values)):
            packed_row[index : index + 1, here] = packed[index, group : group + 1, :]
    row_hit = lax.broadcasted_iota(jnp.int32, (groups, live), 0) == (place_row[...] >> 7)
    low_hit = jnp.where(
        lax.broadcasted_iota(jnp.int32, (LANES, live), 0) == (place_row[...] & 127), 1.0, 0.0
    ).astype(BF16)
    pieces = [
        jnp.where(row_hit, packed_row[index : index + 1, :], 0.0).astype(BF16)
        for index in range(len(values))
    ]
    spread = product_lanes(jnp.concatenate(pieces, axis=0), low_hit)
    placed = [
        (spread[first : first + groups] + spread[first + groups : first + 2 * groups])
        + spread[first + 2 * groups : first + 3 * groups]
        for first in (0, 3 * groups)
    ]
    column_scale[...] = placed[1]
    for group in range(groups):
        pole_wide[group * LANES : (group + 1) * LANES, :] = jnp.broadcast_to(
            placed[0][group : group + 1, :], (LANES, LANES)
        ).T

    blocks = root_gap.shape[0] // parts
    mine = blocks * LANES
    for block in range(blocks):
        here = slice(block * LANES, (block + 1) * LANES)
        row = pl.ds(block * parts + core[0], 1)
        gaps[:, here] = root_gap[row, :]
        rows[1:2, here] = root_offset[row, :]
    own_row = pl.ds(position[0] * parts + core[0], 1)
    gaps[:, mine : mine + LANES] = root_gap[own_row, :]
    count = gaps.shape[1]
    hit = jnp.where(
        lax.broadcasted_iota(jnp.int32, (groups, count), 0) == (gaps[...] >> 7), 1.0, 0.0
    ).astype(BF16)
    near = None
    for piece in split_three(pole_values[:groups]):
        part = lax.dot_general(
            piece, hit, (((0,), (0,)), ((), ())), preferred_element_type=F32
        )
        near = part if near is None else near + part
    chosen = lax.broadcasted_iota(jnp.int32, (LANES, count), 0) == (gaps[...] & 127)
    base = jnp.sum(jnp.where(chosen, near, 0.0), axis=0, keepdims=True)
    rows[0:1, :] = base[:, :mine]
    base_tall = jnp.broadcast_to(base[:, mine : mine + LANES], (LANES, LANES)).T
    offset_tall = jnp.broadcast_to(root_offset[own_row, :], (LANES, LANES)).T
    total = jnp.zeros((LANES, LANES), F32)
    for group in range(groups):
        gap = (pole_values[group : group + 1, :] - base_tall) - offset_tall
        entry = coupling_live[group : group + 1, :] * inverse_of(gap)
        total = total + entry * entry
    root_scale[...] = lax.rsqrt(jnp.sum(total.T, axis=0, keepdims=True) + EPSILON)


def merge_kernel(core, mine, other, column_scale, pole_wide, rows, out, pieces, held, sems):
    groups, band, width = mine.shape
    quarter = groups // 4
    copies = []
    for index in range(4):
        block = pl.ds(index * quarter, quarter)
        copies.append(pltpu.make_async_copy(other.at[block], held.at[block], sems.at[index]))
        copies[index].start()
    parts = width // LANES
    depth = groups * width
    tiles = rows.shape[1] // ROOT_TILE
    per_tile = ROOT_TILE // LANES
    for half, ref in enumerate((mine, held)):
        for source in range(groups):
            if half == 1 and source % quarter == 0:
                copies[source // quarter].wait()
            for part in range(parts):
                lanes = slice(part * LANES, (part + 1) * LANES)
                first = source * width + part * LANES
                at = slice(first, first + LANES)
                row = source * parts + part
                high, low = split_two(ref[source, :, lanes] * column_scale[row : row + 1, :])
                pieces[half * band : (half + 1) * band, at] = high
                pieces[(2 + half) * band : (3 + half) * band, at] = low

    def one_tile(tile, carry):
        first = tile * ROOT_TILE
        base_row = rows[0:1, pl.ds(first, ROOT_TILE)]
        offset_row = rows[1:2, pl.ds(first, ROOT_TILE)]
        total = None
        for start in range(0, depth, CHUNK):
            column = pole_wide[start : start + CHUNK, :]
            highs = []
            lows = []
            for part in range(per_tile):
                lanes = slice(part * LANES, (part + 1) * LANES)
                gap = (column - base_row[:, lanes]) - offset_row[:, lanes]
                high = pltpu.reciprocal(gap, approx=True).astype(BF16)
                lows.append((1.0 - gap * high.astype(F32)).astype(BF16) * high)
                highs.append(high)
            both = product(pieces[:, start : start + CHUNK], jnp.concatenate(highs, axis=1))
            rest = product(
                pieces[: 2 * band, start : start + CHUNK], jnp.concatenate(lows, axis=1)
            )
            part = both[: 2 * band] + both[2 * band :] + rest
            total = part if total is None else total + part
        for half, which in enumerate((core[0], 1 - core[0])):
            for part in range(per_tile):
                lanes = slice(part * LANES, (part + 1) * LANES)
                block = which * groups + tile * per_tile + part
                out[block] = total[half * band : (half + 1) * band, lanes]
        return carry

    for tile in range(tiles):
        one_tile(tile, 0)


def finish_kernel(core, blocks, scale_mine, scale_other, merged, made, sems):
    sources, band, width = blocks.shape
    groups = sources // 2
    pieces = sems.shape[1]
    step = groups // pieces
    copies = []
    for half in range(2):
        rows = pl.ds(half * width, width)
        scale = jnp.where(core[0] == half, scale_mine[...], scale_other[...])
        for piece in range(pieces):
            first = half * groups + piece * step
            tall = blocks[first : first + step].reshape(step * band, width)
            lanes = pl.ds(piece * step * band, step * band)
            made[rows, lanes] = (tall * scale).T
            copies.append(
                pltpu.make_async_copy(
                    made.at[rows, lanes], merged.at[rows, lanes], sems.at[half, piece]
                )
            )
            copies[-1].start()
    for copy in copies:
        copy.wait()


def hbm(count):
    return [pl.BlockSpec(memory_space=pltpu.HBM)] * count


def vmem(count):
    return [pl.BlockSpec(memory_space=pltpu.VMEM)] * count


def per_device(
    children, permutation, type_counts, rotation, pole_values, coupling, root_gap, root_offset
):
    order_size = permutation.shape[0]
    half_size = order_size // 2
    groups = lax.axis_size("col")
    position = lax.axis_index("col")
    row_index = lax.axis_index("row")
    rows = lax.axis_size("row")
    core = row_index % 2
    is_upper = row_index < rows // 2
    root_count = root_gap.shape[0]
    share = root_count // groups
    band = children.shape[0] // groups
    width = children.shape[1]
    pairs = [(index, index ^ 1) for index in range(rows)]

    mine = lax.all_to_all(
        children.reshape(groups, band, width), "col", split_axis=0, concat_axis=0, tiled=True
    )
    mine, permutation = lax.optimization_barrier((mine, permutation))
    other = lax.ppermute(mine, "row", pairs)
    column_scale, pole_wide, root_rows, root_scale = pl.pallas_call(
        prep_kernel,
        out_shape=(
            jax.ShapeDtypeStruct((half_size // LANES, LANES), F32),
            jax.ShapeDtypeStruct((half_size, LANES), F32),
            jax.ShapeDtypeStruct((2, root_count // 2), F32),
            jax.ShapeDtypeStruct((1, LANES), F32),
        ),
        in_specs=[pl.BlockSpec(memory_space=pltpu.SMEM)] * 5 + vmem(6),
        out_specs=tuple(vmem(4)),
        scratch_shapes=[
            pltpu.VMEM((half_size // LANES, LANES), F32),
            pltpu.VMEM((6, half_size // LANES, LANES), F32),
            pltpu.VMEM((6, half_size), F32),
            pltpu.VMEM((1, half_size), jnp.int32),
            pltpu.VMEM((1, root_count // 2 + LANES), jnp.int32),
        ],
        compiler_params=pltpu.CompilerParams(vmem_limit_bytes=32 * 2**20),
        cost_estimate=pl.CostEstimate(
            flops=4 * 10**9, bytes_accessed=4 * 10**6, transcendentals=2 * 10**6
        ),
    )(
        type_counts,
        core.reshape(1),
        position.reshape(1),
        row_index.reshape(1),
        jnp.full((1,), rows, jnp.int32),
        *(
            value.reshape(-1, LANES)
            for value in (permutation, rotation, pole_values, coupling, root_gap, root_offset)
        ),
    )
    other_scale = lax.ppermute(root_scale, "row", pairs)
    blocks = pl.pallas_call(
        merge_kernel,
        out_shape=jax.ShapeDtypeStruct((2 * groups, band, share // 2), F32),
        in_specs=[pl.BlockSpec(memory_space=pltpu.SMEM)] + vmem(1) + hbm(1) + vmem(3),
        out_specs=vmem(1)[0],
        scratch_shapes=[
            pltpu.VMEM((4 * band, groups * width), BF16),
            pltpu.VMEM((groups, band, width), F32),
            pltpu.SemaphoreType.DMA((4,)),
        ],
        compiler_params=pltpu.CompilerParams(vmem_limit_bytes=32 * 2**20),
        cost_estimate=pl.CostEstimate(
            flops=30 * 10**9, bytes_accessed=10 * 10**6, transcendentals=12 * 10**6
        ),
    )(core.reshape(1), mine, other, column_scale, pole_wide, root_rows)
    blocks, other_scale = lax.optimization_barrier((blocks, other_scale))
    chips = [
        [(pair * 2 + half) * groups + index for half in range(2) for index in range(groups)]
        for pair in range(rows // 2)
    ]
    blocks = lax.all_to_all(
        blocks, ("row", "col"), split_axis=0, concat_axis=0, axis_index_groups=chips, tiled=True
    )
    return pl.pallas_call(
        finish_kernel,
        out_shape=jax.ShapeDtypeStruct((share, groups * band), F32),
        in_specs=[pl.BlockSpec(memory_space=pltpu.SMEM)] + vmem(3),
        out_specs=hbm(1)[0],
        scratch_shapes=[
            pltpu.VMEM((share, groups * band), F32),
            pltpu.SemaphoreType.DMA((2, 4)),
        ],
        compiler_params=pltpu.CompilerParams(vmem_limit_bytes=16 * 2**20),
    )(core.reshape(1), blocks, root_scale, other_scale)


def solution(mesh):
    placed = (P("row", "col"), P(), P(), P(), P(), P(), P(), P())
    return jax.shard_map(
        per_device, mesh=mesh, in_specs=placed, out_specs=P("col", "row"), check_vma=False
    )
```
